32 devices in a mesh: req: 8 (over z, y), mp: 4 (over x, core).
Axes of the slice: x: 2, y: 2, z: 4, core: 2. Of those that a mesh axis runs over, the one named last changes fastest.
Arguments:
- queries: bfloat16 [4, 64, 4096], P(None, 'req', 'mp'), may hold values from -1200 to 1200
- fresh_key_value: bfloat16 [4, 2, 64, 2048], P(None, None, 'req', 'mp'), may hold values from -6 to 6
- suffix_key_value: bfloat16 [2, 64, 128, 2048], P(None, 'req', None, 'mp'), may hold values from -6 to 6
- suffix_len: int32 [64], P('req'), may hold values from 1 to 128
- prefix_ids: int32 [64], P('req'), may hold values from 0 to 3
- panel_owner: int32 [8], P('req'), may hold values from 0 to 7, each once
- prefix_key_value: bfloat16 [2, 8, 2048, 2048], P(None, 'req', None, 'mp'), may hold values from -6 to 6
- out_weight: bfloat16 [4096, 4608], P('mp'), may hold values from -0.09375 to 0.09375
- swap_flags: int32 [4, 64], P(None, 'req'), may hold values from 0 to 1, as said below
Outputs:
- attn_out: bfloat16 [4, 64, 4608], P(None, 'req', 'mp')
The draws below stay inside these ranges and needn't reach their ends.
Inputs may be any that keep to these rules, and one draw needn't show every extreme that they name: `swap_flags`: in each step exactly 2 slots of every device are flagged, and a device and its partner of that step flag the same slots.
All inputs are finite; a program needn't handle non-finite values.
Results may differ from the reference program's by a relative error of at most 0.0057.
Values may be sent and summed in bfloat16 or wider, within the bound.
A program may use at most 384 MiB of HBM per device.

```python
import math
import jax
import jax.numpy as jnp
import numpy as np
from jax import lax

D = 4608
QUERY_HEADS = 32
KEY_VALUE_HEADS = 16
HEAD_DIMENSION = 128
REQUESTS_PER_RANK = 8
SUFFIX_SLOTS = 128
PANEL_TOKENS = 2048
DECODE_STEPS = 4
SWAP_SLOTS = 2
REQUEST_COUNT = 64
PREFIXES = 4
N_REQ = 8


def draw_queries(key, part):
    key = jax.random.fold_in(key, 11)
    values = jnp.clip(jax.random.normal(key, (DECODE_STEPS, REQUEST_COUNT, QUERY_HEADS * HEAD_DIMENSION), jnp.float32), -6.0, 6.0)
    return values.astype(jnp.bfloat16)


def draw_swap_flags(key, part):
    key = jax.random.fold_in(key, 7)
    device_ids = jnp.arange(N_REQ, dtype=jnp.int32)
    slot_ids = jnp.arange(REQUESTS_PER_RANK, dtype=jnp.int32)
    bit_count = N_REQ.bit_length() - 1
    chosen_rows = []
    for decode_step_index in range(DECODE_STEPS):
        pair_bit = 1 << decode_step_index % bit_count
        leader = jnp.bitwise_and(device_ids, N_REQ - 1 - pair_bit)
        raw_scores = jax.random.randint(jax.random.fold_in(key, decode_step_index), (N_REQ, REQUESTS_PER_RANK), 0, 1 << 20) * REQUESTS_PER_RANK + slot_ids[None, :]
        ranks = jnp.argsort(jnp.argsort(raw_scores, axis=1), axis=1)
        chosen = (ranks < SWAP_SLOTS).astype(jnp.int32)
        chosen_rows.append(chosen[leader].reshape(-1))
    return jnp.stack(chosen_rows).astype(jnp.int32)


def plant(entries, key, smallest, largest):
    extent = entries.shape
    place = [jax.random.randint(jax.random.fold_in(key, axis), (), 0, extent[axis]) for axis in range(len(extent))]
    entries = entries.at[tuple(place)].set(smallest)
    longest = extent.index(max(extent))
    place[longest] = (place[longest] + 1) % extent[longest]
    return entries.at[tuple(place)].set(largest)


def levels(key, dims, cuts, low, high):
    def one(axis_at, blocks):
        heights = jax.random.uniform(jax.random.fold_in(jax.random.fold_in(key, 6), axis_at), (blocks,), jnp.float32, low / len(cuts), high / len(cuts))
        return jnp.repeat(jnp.exp(heights), dims[axis_at] // blocks).reshape((-1,) + (1,) * (len(dims) - axis_at - 1))

    loudness = one(*cuts[0])
    for cut in cuts[1:]:
        loudness = loudness * one(*cut)
    return loudness


def rank_bounds(count, slope):
    weights = [(1 << 20) // math.isqrt(grade ** slope) + 1 for grade in range(1, count + 1)]
    deviation = 1 + sum(weights) // (1 << 30)
    return np.cumsum(np.array([max(1, weight // deviation) for weight in weights]))


def ranked_ids(key, extent, number_of, skew):
    table = rank_bounds(number_of, skew)
    lot = jax.random.randint(jax.random.fold_in(key, 1), extent, 0, int(table[number_of - 1]))
    grade = jnp.searchsorted(jnp.asarray(table, jnp.int32), lot, side="right")
    return jax.random.permutation(jax.random.fold_in(key, 2), number_of)[grade].astype(jnp.int32)


def noise(stream_key, dims, spread, bound, cuts=(), kind=jnp.bfloat16):
    entries = spread * jax.random.normal(stream_key, dims, jnp.float32)
    if cuts:
        entries = entries * levels(stream_key, dims, cuts, -0.22, 0.18)
    return jnp.clip(entries, -bound, bound).astype(kind)


def setup_inputs(seed: int = 0) -> dict:
    key_list = jax.random.split(jax.random.key(seed), 10)
    queries = draw_queries(jax.random.fold_in(key_list[9], 71), 0)
    fresh_key_value = noise(key_list[1], (DECODE_STEPS, 2, REQUEST_COUNT, KEY_VALUE_HEADS * HEAD_DIMENSION), 1.0, 6.0, ((2, 8), (3, 4)))
    suffix_key_value = noise(key_list[2], (2, REQUEST_COUNT, SUFFIX_SLOTS, KEY_VALUE_HEADS * HEAD_DIMENSION), 1.0, 6.0, ((1, 8), (3, 4)))
    suffix_len = plant(jax.random.randint(key_list[3], (REQUEST_COUNT,), 1, SUFFIX_SLOTS + 1), jax.random.fold_in(key_list[3], 1), 1, SUFFIX_SLOTS).astype(jnp.int32)
    prefix_ids = plant(ranked_ids(key_list[4], (REQUEST_COUNT,), PREFIXES, 2), jax.random.fold_in(key_list[4], 3), 0, PREFIXES - 1).astype(jnp.int32)
    panel_owner = jax.random.permutation(key_list[5], N_REQ).astype(jnp.int32)
    prefix_key_value = noise(key_list[6], (2, N_REQ, PANEL_TOKENS, KEY_VALUE_HEADS * HEAD_DIMENSION), 1.0, 6.0, ((1, 8), (3, 4)))
    out_weight = noise(key_list[7], (QUERY_HEADS * HEAD_DIMENSION, D), (QUERY_HEADS * HEAD_DIMENSION) ** -0.5, 0.09375, ((0, 4),))
    swap_flags = draw_swap_flags(jax.random.fold_in(key_list[9], 71), 0)
    return dict(queries=queries, fresh_key_value=fresh_key_value, suffix_key_value=suffix_key_value, suffix_len=suffix_len, prefix_ids=prefix_ids, panel_owner=panel_owner, prefix_key_value=prefix_key_value, out_weight=out_weight, swap_flags=swap_flags)


NEG = -1.0e30


def block_stats(scores, is_valid, values_block, pattern):
    masked = jnp.where(is_valid, scores, NEG)
    peak_value = jnp.max(masked, axis=-1)
    weights = jnp.where(is_valid, jnp.exp(masked - peak_value[..., None]), 0.0).astype(jnp.bfloat16)
    weights_wide = weights.astype(jnp.float32)
    total = jnp.sum(weights_wide, axis=-1)
    summed = jnp.einsum(pattern, weights_wide, values_block.astype(jnp.float32))
    return peak_value, total, summed


def reference(queries, fresh_key_value, suffix_key_value, suffix_len, prefix_ids, panel_owner, prefix_key_value, out_weight, swap_flags):
    query_group_count = QUERY_HEADS // KEY_VALUE_HEADS
    score_scale = (D // QUERY_HEADS) ** -0.5
    bit_count = N_REQ.bit_length() - 1
    device_ids = jnp.arange(N_REQ, dtype=jnp.int32)
    slot_ids = jnp.arange(REQUESTS_PER_RANK, dtype=jnp.int32)
    request_suffix_cache = suffix_key_value
    past_tokens = jnp.zeros((2, REQUEST_COUNT, DECODE_STEPS, KEY_VALUE_HEADS * HEAD_DIMENSION), jnp.bfloat16)
    lengths = suffix_len
    prefix_of = prefix_ids
    position = jnp.arange(SUFFIX_SLOTS + DECODE_STEPS, dtype=jnp.int32)
    results = []
    for decode_step_index in range(DECODE_STEPS):
        partner = jnp.bitwise_xor(device_ids, 1 << (decode_step_index % bit_count))
        source = (partner[:, None] * REQUESTS_PER_RANK + slot_ids[None, :]).reshape(-1).astype(jnp.int32)
        is_moved = swap_flags[decode_step_index] == 1
        request_suffix_cache = jnp.where(is_moved[None, :, None, None], jnp.take(request_suffix_cache, source, axis=1), request_suffix_cache)
        past_tokens = jnp.where(is_moved[None, :, None, None], jnp.take(past_tokens, source, axis=1), past_tokens)
        lengths = jnp.where(is_moved, jnp.take(lengths, source), lengths)
        prefix_of = jnp.where(is_moved, jnp.take(prefix_of, source), prefix_of)
        past_tokens = past_tokens.at[:, :, decode_step_index].set(fresh_key_value[decode_step_index])
        query_matrix = queries[decode_step_index].astype(jnp.float32).reshape(REQUEST_COUNT, KEY_VALUE_HEADS, query_group_count, HEAD_DIMENSION)

        def own_block(items):
            query_block, cache_tile, past_token_block, length_block = items
            request_keys = jnp.concatenate([cache_tile[0], past_token_block[0]], axis=1).reshape(REQUESTS_PER_RANK, SUFFIX_SLOTS + DECODE_STEPS, KEY_VALUE_HEADS, HEAD_DIMENSION)
            request_values = jnp.concatenate([cache_tile[1], past_token_block[1]], axis=1).reshape(REQUESTS_PER_RANK, SUFFIX_SLOTS + DECODE_STEPS, KEY_VALUE_HEADS, HEAD_DIMENSION)
            scores = jnp.einsum('rkgd,rtkd->rkgt', query_block, request_keys.astype(jnp.float32)) * score_scale
            is_valid = jnp.where(position[None, :] < SUFFIX_SLOTS, position[None, :] < length_block[:, None], position[None, :] - SUFFIX_SLOTS <= decode_step_index)
            return block_stats(scores, is_valid[:, None, None, :], request_values, 'rkgt,rtkd->rkgd')

        request_maximum, request_denominator_sum, request_weighted_sum = lax.map(own_block, (
            query_matrix.reshape(N_REQ, REQUESTS_PER_RANK, KEY_VALUE_HEADS, query_group_count, HEAD_DIMENSION),
            request_suffix_cache.reshape(2, N_REQ, REQUESTS_PER_RANK, SUFFIX_SLOTS, KEY_VALUE_HEADS * HEAD_DIMENSION).transpose(1, 0, 2, 3, 4),
            past_tokens.reshape(2, N_REQ, REQUESTS_PER_RANK, DECODE_STEPS, KEY_VALUE_HEADS * HEAD_DIMENSION).transpose(1, 0, 2, 3, 4),
            lengths.reshape(N_REQ, REQUESTS_PER_RANK)))
        request_maximum = request_maximum.reshape(REQUEST_COUNT, KEY_VALUE_HEADS, query_group_count)
        request_denominator_sum = request_denominator_sum.reshape(REQUEST_COUNT, KEY_VALUE_HEADS, query_group_count)
        request_weighted_sum = request_weighted_sum.reshape(REQUEST_COUNT, KEY_VALUE_HEADS, query_group_count, HEAD_DIMENSION)

        def panel_block(rank_index):
            shared_panel_keys = prefix_key_value[0, rank_index].astype(jnp.float32).reshape(PANEL_TOKENS, KEY_VALUE_HEADS, HEAD_DIMENSION)
            shared_panel_values = prefix_key_value[1, rank_index].reshape(PANEL_TOKENS, KEY_VALUE_HEADS, HEAD_DIMENSION)
            matched = prefix_of == panel_owner[rank_index] // 2
            scores = jnp.einsum('rkgd,tkd->rkgt', query_matrix, shared_panel_keys) * score_scale
            return block_stats(scores, matched[:, None, None, None], shared_panel_values, 'rkgt,tkd->rkgd')

        panel_peak, panel_total, panel_sum = lax.map(panel_block, jnp.arange(N_REQ, dtype=jnp.int32))
        overall = jnp.maximum(request_maximum, jnp.max(panel_peak, axis=0))
        own_factor = jnp.exp(request_maximum - overall)
        panel_factor = jnp.exp(panel_peak - overall[None])
        numerator = request_weighted_sum * own_factor[..., None] + jnp.sum(panel_sum * panel_factor[..., None], axis=0)
        denominator = request_denominator_sum * own_factor + jnp.sum(panel_total * panel_factor, axis=0)
        attended = (numerator / denominator[..., None]).reshape(REQUEST_COUNT, QUERY_HEADS * HEAD_DIMENSION).astype(jnp.bfloat16)
        results.append(attended)
    stacked = jnp.stack(results).reshape(DECODE_STEPS * REQUEST_COUNT, QUERY_HEADS * HEAD_DIMENSION)
    projected = jnp.dot(stacked, out_weight, preferred_element_type=jnp.float32)
    return projected.reshape(DECODE_STEPS, REQUEST_COUNT, D).astype(jnp.bfloat16)
```

```python
import functools
import math

import jax
import jax.numpy as jnp
from jax import lax
from jax.experimental import pallas as pl
from jax.experimental.pallas import tpu as pltpu
from jax.sharding import PartitionSpec as P

D = 4608
QUERY_HEADS = 32
HEAD_DIMENSION = 128
SUFFIX_SLOTS = 128
PANEL_TOKENS = 2048
DECODE_STEPS = 4
BLOCK_RANKS = 4

NEG = -1e30
EXP2_SCALE = (D // QUERY_HEADS) ** (-0.5) * math.log2(math.e)
MESH = pl.DeviceIdType.MESH
F32 = jnp.float32
BF16 = jnp.bfloat16


def dot_t(left, right):
    return lax.dot_general(left, right, (((1,), (1,)), ((), ())), preferred_element_type=F32)


def iota(shape, dimension):
    return lax.broadcasted_iota(jnp.int32, shape, dimension)


def block_stats(queries, keys, values, is_valid):
    scores = dot_t(queries, keys)
    if is_valid is not None:
        scores = jnp.where(is_valid, scores, NEG)
    peak = jnp.max(scores, axis=1, keepdims=True)
    weights = jnp.exp2((scores - peak) * EXP2_SCALE)
    if is_valid is not None:
        weights = jnp.where(is_valid, weights, 0.0)
    widened = jnp.concatenate([values, jnp.ones(values.shape, BF16)], axis=1)
    summed = jnp.dot(weights.astype(BF16), widened, preferred_element_type=F32)
    return peak, summed[:, :HEAD_DIMENSION], summed[:, HEAD_DIMENSION:]


def kernel(
    n_req,
    n_mp,
    q_hbm,
    fresh_hbm,
    suffix_hbm,
    mask_hbm,
    info_hbm,
    panel_hbm,
    weight_hbm,
    out_ref,
    q_all,
    info_all,
    panel,
    suffix,
    fresh,
    mask,
    weight,
    num_out,
    stat_out,
    num_in,
    stat_in,
    attended,
    part_out,
    part_in,
    local_sem,
    q_send,
    q_recv,
    info_send,
    info_recv,
    num_send,
    num_recv,
    stat_send,
    stat_recv,
    part_send,
    part_recv,
):
    me = lax.axis_index("req")
    mp = lax.axis_index("mp")
    half = n_req // 2
    side = me // half
    place = me % half
    near_base = side * half
    far_base = (1 - side) * half
    kv_local = panel.shape[2] // HEAD_DIMENSION
    rows_rank = q_all.shape[1]
    slots = rows_rank // DECODE_STEPS
    rows = BLOCK_RANKS * rows_rank
    lanes = info_all.shape[2]

    local = [
        pltpu.make_async_copy(q_hbm, q_all.at[me], local_sem.at[0]),
        pltpu.make_async_copy(info_hbm, info_all.at[me], local_sem.at[1]),
        pltpu.make_async_copy(panel_hbm, panel, local_sem.at[2]),
        pltpu.make_async_copy(fresh_hbm, fresh, local_sem.at[3]),
        pltpu.make_async_copy(suffix_hbm, suffix, local_sem.at[4]),
        pltpu.make_async_copy(mask_hbm, mask, local_sem.at[5]),
        pltpu.make_async_copy(weight_hbm, weight, local_sem.at[6]),
    ]
    for copy in local:
        copy.start()

    near = [
        (d, near_base + (place + d) % half, near_base + (place + half - d) % half)
        for d in range(1, half)
    ]
    far = [
        (half + d, far_base + (place + d) % half, far_base + (place + half - d) % half)
        for d in range(half)
    ]
    mp_peers = [(d, (mp + d) % n_mp, (mp + n_mp - d) % n_mp) for d in range(1, n_mp)]
    mp_peers = sorted(mp_peers, key=lambda peer: abs(peer[0] - n_mp // 2))

    barrier = pltpu.get_barrier_semaphore()
    for _, target, _ in near + far:
        pl.semaphore_signal(barrier, inc=1, device_id=(target, mp), device_id_type=MESH)
    for _, target, _ in mp_peers:
        pl.semaphore_signal(barrier, inc=1, device_id=(me, target), device_id_type=MESH)
    pl.semaphore_wait(barrier, n_req - 1 + n_mp - 1)

    def remote(source, destination, send, receive, index, device):
        return pltpu.make_async_remote_copy(
            src_ref=source,
            dst_ref=destination,
            send_sem=send.at[index],
            recv_sem=receive.at[index],
            device_id=device,
            device_id_type=MESH,
        )

    def query_copy(index, target, slot):
        return remote(q_hbm, q_all.at[slot], q_send, q_recv, index, (target, mp))

    def info_copy(index, target, slot):
        return remote(info_hbm, info_all.at[slot], info_send, info_recv, index, (target, mp))

    def num_copy(index, target, slot):
        return remote(
            num_out.at[target], num_in.at[slot], num_send, num_recv, index, (target, mp)
        )

    def stat_copy(index, target, slot):
        return remote(
            stat_out.at[target], stat_in.at[slot], stat_send, stat_recv, index, (target, mp)
        )

    def part_copy(index, target, slot):
        return remote(
            part_out.at[target], part_in.at[slot], part_send, part_recv, index, (me, target)
        )

    for index, target, _ in near + far:
        info_copy(index, target, me).start()
    for index, target, _ in near + far:
        query_copy(index, target, me).start()

    local[1].wait()
    local[5].wait()
    for index, target, source in near + far:
        info_copy(index, target, source).wait_recv()
    info = info_all[0]
    for rank in range(1, n_req):
        info = info + info_all[rank]
    state_row = iota((8, lanes), 0)
    position = iota((8, lanes), 1)
    state = jnp.where(
        state_row == 0,
        position.astype(F32),
        jnp.where(state_row == 1, jnp.broadcast_to(info[4:5], (8, lanes)), 0.0),
    )
    bit_count = n_req.bit_length() - 1
    requests = jnp.zeros((8, lanes), F32)
    for step in range(DECODE_STEPS):
        distance = slots << (step % bit_count)
        lane = iota((lanes, lanes), 1)
        partner = jnp.where((lane // distance) % 2 == 1, lane - distance, lane + distance)
        flag = jnp.broadcast_to(info[step : step + 1], (lanes, lanes)) > 0.5
        origin = jnp.where(flag, partner, lane)
        moves = jnp.where(iota((lanes, lanes), 0) == origin, 1.0, 0.0).astype(BF16)
        state = jnp.dot(state.astype(BF16), moves, preferred_element_type=F32)
        requests = jnp.where(state_row == step, state[0:1], requests)
        requests = jnp.where(state_row == DECODE_STEPS + step, state[1:2], requests)
    requests = requests.astype(BF16)
    token = iota((rows_rank, lanes), 0)
    token_at = jnp.where(iota((rows_rank, lanes), 1) == me * slots + token % slots, 1.0, 0.0)
    token_steps = dot_t(requests, token_at.astype(BF16))
    token_step = iota((1, rows_rank), 1) // slots
    token_request = jnp.zeros((1, rows_rank), F32)
    for step in range(DECODE_STEPS):
        token_request = jnp.where(token_step == step, token_steps[step : step + 1], token_request)
    my_prefix = mask[slots : slots + 1, 0:1]

    def work(first):
        row = iota((rows, lanes), 0)
        row_position = (first + row // rows_rank) * slots + row % slots
        row_at = jnp.where(iota((rows, lanes), 1) == row_position, 1.0, 0.0).astype(BF16)
        down = dot_t(row_at, requests)
        across = dot_t(requests, row_at)
        down_step = (iota((rows, 1), 0) // slots) % DECODE_STEPS
        across_step = (iota((1, rows), 1) // slots) % DECODE_STEPS
        down_request = jnp.zeros((rows, 1), F32)
        down_prefix = jnp.zeros((rows, 1), F32)
        across_request = jnp.zeros((1, rows), F32)
        for step in range(DECODE_STEPS):
            here = down_step == step
            down_request = jnp.where(here, down[:, step : step + 1], down_request)
            down_prefix = jnp.where(
                here, down[:, DECODE_STEPS + step : DECODE_STEPS + step + 1], down_prefix
            )
            across_request = jnp.where(across_step == step, across[step : step + 1], across_request)
        matched = jnp.where(down_prefix == my_prefix, 1.0, 0.0)
        matched = jnp.concatenate([matched, matched], axis=0) > 0.5
        own = iota((rows_rank, rows), 0)
        pick = jnp.where(
            (across_request == (me * slots + own % slots).astype(F32))
            & (across_step == own // slots),
            1.0,
            0.0,
        ).astype(BF16)
        own = iota((rows, rows_rank), 1)
        put = jnp.where(
            (down_request == (me * slots + own % slots).astype(F32)) & (down_step == own // slots),
            1.0,
            0.0,
        )
        is_here = jnp.sum(put, axis=1, keepdims=True)
        is_here = jnp.concatenate([is_here, is_here], axis=0) > 0.5
        fresh_valid = jnp.where(
            (down_request == token_request) & (down_step >= token_step), 1.0, 0.0
        )
        fresh_valid = jnp.concatenate([fresh_valid, fresh_valid], axis=0) > 0.5

        def head(h, carry):
            at = pl.ds(pl.multiple_of(h * HEAD_DIMENSION, HEAD_DIMENSION), HEAD_DIMENSION)
            pair = [
                pl.ds(
                    pl.multiple_of((2 * h + g) * HEAD_DIMENSION, HEAD_DIMENSION), HEAD_DIMENSION
                )
                for g in range(2)
            ]
            query = [
                q_all[pl.ds(first, BLOCK_RANKS), :, pair[g]].reshape(rows, HEAD_DIMENSION)
                for g in range(2)
            ]
            both = jnp.concatenate(query, axis=0)
            panel_peak, panel_num, panel_den = block_stats(
                both, panel[0, :, at], panel[1, :, at], None
            )
            panel_peak = jnp.where(matched, panel_peak, NEG)
            own_query = jnp.concatenate(
                [jnp.dot(pick, part, preferred_element_type=F32) for part in query], axis=0
            ).astype(BF16)
            slot_valid = mask[0:slots]
            slot_valid = jnp.concatenate([slot_valid] * (2 * DECODE_STEPS), axis=0) > 0.5
            tokens = suffix.shape[1] * suffix.shape[2]
            own_peak, own_num, own_den = block_stats(
                own_query,
                suffix[0, :, :, at].reshape(tokens, HEAD_DIMENSION),
                suffix[1, :, :, at].reshape(tokens, HEAD_DIMENSION),
                slot_valid,
            )
            own_all = jnp.concatenate(
                [own_num, own_den, jnp.broadcast_to(own_peak, own_num.shape)], axis=1
            )
            own_all = jnp.concatenate(
                [
                    jnp.dot(
                        put,
                        own_all[g * rows_rank : (g + 1) * rows_rank],
                        preferred_element_type=F32,
                        precision=lax.Precision.HIGHEST,
                    )
                    for g in range(2)
                ],
                axis=0,
            )
            own_num = own_all[:, :HEAD_DIMENSION]
            own_den = own_all[:, HEAD_DIMENSION : 2 * HEAD_DIMENSION]
            own_peak = jnp.where(is_here, own_all[:, 2 * HEAD_DIMENSION :], NEG)
            fresh_peak, fresh_num, fresh_den = block_stats(
                both, fresh[0, :, at], fresh[1, :, at], fresh_valid
            )
            peak = jnp.maximum(jnp.maximum(panel_peak, fresh_peak), own_peak)
            panel_factor = jnp.where(matched, jnp.exp2((panel_peak - peak) * EXP2_SCALE), 0.0)
            own_factor = jnp.exp2((own_peak - peak) * EXP2_SCALE)
            fresh_factor = jnp.exp2((fresh_peak - peak) * EXP2_SCALE)
            num = panel_num * panel_factor + own_num * own_factor + fresh_num * fresh_factor
            den = panel_den * panel_factor + own_den * own_factor + fresh_den * fresh_factor
            lane = iota((rows, HEAD_DIMENSION), 1)
            held = stat_out[pl.ds(first, BLOCK_RANKS)].reshape(rows, HEAD_DIMENSION)
            for g in range(2):
                part = slice(g * rows, (g + 1) * rows)
                held = jnp.where(lane == 2 * h + g, peak[part], held)
                held = jnp.where(lane == 64 + 2 * h + g, den[part], held)
                num_out[pl.ds(first, BLOCK_RANKS), :, pair[g]] = (
                    num[part].astype(BF16).reshape(BLOCK_RANKS, rows_rank, HEAD_DIMENSION)
                )
            stat_out[pl.ds(first, BLOCK_RANKS)] = held.reshape(
                BLOCK_RANKS, rows_rank, HEAD_DIMENSION
            )
            return carry

        lax.fori_loop(0, kv_local, head, 0)

    stat_out[...] = jnp.zeros(stat_out.shape, F32)
    local[0].wait()
    for index, target, source in near:
        query_copy(index, target, source).wait_recv()
    for copy in local[2:5]:
        copy.wait()
    for block in range(half // BLOCK_RANKS):
        work(near_base + block * BLOCK_RANKS)
    for index, target, _ in near:
        stat_copy(index, target, me).start()
        num_copy(index, target, me).start()
    for index, target, source in far:
        query_copy(index, target, source).wait_recv()
    for block in range(half // BLOCK_RANKS):
        work(far_base + block * BLOCK_RANKS)
    for index, target, _ in far:
        stat_copy(index, target, me).start()
        num_copy(index, target, me).start()
    num_in[me] = num_out[me]
    stat_in[me] = stat_out[me]
    for index, target, source in near + far:
        stat_copy(index, target, source).wait_recv()
        num_copy(index, target, source).wait_recv()

    peak = stat_in[0]
    for rank in range(1, n_req):
        peak = jnp.maximum(peak, stat_in[rank])
    factors = [jnp.exp2((stat_in[rank] - peak) * EXP2_SCALE) for rank in range(n_req)]
    total = jnp.zeros(peak.shape, F32)
    for rank in range(n_req):
        total = total + factors[rank] * pltpu.roll(stat_in[rank], 64, 1)
    head_lanes = iota(peak.shape, 1) < 2 * kv_local
    total = jnp.where(head_lanes, total, 1.0)
    factors = [jnp.where(head_lanes, factor, 0.0) / total for factor in factors]
    for h in range(2 * kv_local):
        at = slice(h * HEAD_DIMENSION, (h + 1) * HEAD_DIMENSION)
        summed = jnp.zeros((rows_rank, HEAD_DIMENSION), F32)
        for rank in range(n_req):
            summed = summed + factors[rank][:, h : h + 1] * num_in[rank, :, at].astype(F32)
        attended[:, at] = summed.astype(BF16)

    local[6].wait()
    width = out_ref.shape[1]

    def project(target):
        columns = pl.ds(pl.multiple_of(target * width, HEAD_DIMENSION), width)
        return jnp.dot(attended[...], weight[:, columns], preferred_element_type=F32)

    for index, target, _ in mp_peers:
        part_out[target] = project(target).astype(BF16)
        part_copy(index, target, mp).start()
    result = project(mp)
    for index, target, source in mp_peers:
        part_copy(index, target, source).wait_recv()
        result = result + part_in[source].astype(F32)
    out_ref[...] = result.astype(BF16)

    for index, target, source in near + far:
        info_copy(index, target, source).wait_send()
        query_copy(index, target, source).wait_send()
        stat_copy(index, target, source).wait_send()
        num_copy(index, target, source).wait_send()
    for index, target, source in mp_peers:
        part_copy(index, target, source).wait_send()


def shards(
    queries,
    fresh_key_value,
    suffix_key_value,
    suffix_len,
    prefix_ids,
    panel_owner,
    prefix_key_value,
    out_weight,
    swap_flags,
):
    n_req = lax.axis_size("req")
    n_mp = lax.axis_size("mp")
    me = lax.axis_index("req")
    slots = queries.shape[1]
    rows_rank = DECODE_STEPS * slots
    model_lanes = queries.shape[2]
    kv_lanes = suffix_key_value.shape[3]
    width = out_weight.shape[1] // n_mp
    lanes = max(128, n_req * slots)
    info = jnp.concatenate(
        [swap_flags, prefix_ids[None], jnp.zeros((8 - DECODE_STEPS - 1, slots), jnp.int32)]
    ).astype(F32)
    info = jnp.tile(info, (1, lanes // slots))
    info = jnp.where(jnp.arange(lanes)[None] // slots == me, info, 0.0)
    slot = jnp.arange(slots * SUFFIX_SLOTS)[None]
    owner = jnp.arange(slots)[:, None]
    live = (slot // SUFFIX_SLOTS == owner) & (slot % SUFFIX_SLOTS < suffix_len[:, None])
    prefix = jnp.broadcast_to((panel_owner[0] // 2).astype(F32), live.shape)
    mask = jnp.concatenate([live.astype(F32), prefix])
    anywhere = pl.BlockSpec(memory_space=pl.ANY)
    out = pl.pallas_call(
        functools.partial(kernel, n_req, n_mp),
        out_shape=jax.ShapeDtypeStruct((rows_rank, width), BF16),
        in_specs=[anywhere] * 7,
        out_specs=pl.BlockSpec(memory_space=pltpu.VMEM),
        scratch_shapes=[
            pltpu.VMEM((n_req, rows_rank, model_lanes), BF16),
            pltpu.VMEM((n_req, 8, lanes), F32),
            pltpu.VMEM((2, PANEL_TOKENS, kv_lanes), BF16),
            pltpu.VMEM((2, slots, SUFFIX_SLOTS, kv_lanes), BF16),
            pltpu.VMEM((2, rows_rank, kv_lanes), BF16),
            pltpu.VMEM(mask.shape, F32),
            pltpu.VMEM(out_weight.shape, BF16),
            pltpu.VMEM((n_req, rows_rank, model_lanes), BF16),
            pltpu.VMEM((n_req, rows_rank, HEAD_DIMENSION), F32),
            pltpu.VMEM((n_req, rows_rank, model_lanes), BF16),
            pltpu.VMEM((n_req, rows_rank, HEAD_DIMENSION), F32),
            pltpu.VMEM((rows_rank, model_lanes), BF16),
            pltpu.VMEM((n_mp, rows_rank, width), BF16),
            pltpu.VMEM((n_mp, rows_rank, width), BF16),
            pltpu.SemaphoreType.DMA((7,)),
        ]
        + [pltpu.SemaphoreType.DMA((n_req,))] * 8
        + [pltpu.SemaphoreType.DMA((n_mp,))] * 2,
        compiler_params=pltpu.CompilerParams(
            collective_id=0, has_side_effects=True, vmem_limit_bytes=56 * 2**20
        ),
        name="cascade",
    )(
        queries.reshape(rows_rank, model_lanes),
        fresh_key_value.transpose(1, 0, 2, 3).reshape(2, rows_rank, kv_lanes),
        suffix_key_value,
        mask,
        info,
        prefix_key_value.reshape(2, PANEL_TOKENS, kv_lanes),
        out_weight,
    )
    return out.reshape(DECODE_STEPS, slots, width)


def solution(mesh):
    placed = (
        P(None, "req", "mp"),
        P(None, None, "req", "mp"),
        P(None, "req", None, "mp"),
        P("req"),
        P("req"),
        P("req"),
        P(None, "req", None, "mp"),
        P("mp", None),
        P(None, "req"),
    )
    return jax.shard_map(
        shards, mesh=mesh, in_specs=placed, out_specs=P(None, "req", "mp"), check_vma=False
    )
```

```python
import functools
import math

import jax
import jax.numpy as jnp
from jax import lax
from jax.experimental import pallas as pl
from jax.experimental.pallas import tpu as pltpu
from jax.sharding import PartitionSpec as P

D = 4608
QUERY_HEADS = 32
HEAD_DIMENSION = 128
SUFFIX_SLOTS = 128
PANEL_TOKENS = 2048
DECODE_STEPS = 4
BLOCK_RANKS = 4

NEG = -(2.0**100)
EXP2_SCALE = (D // QUERY_HEADS) ** (-0.5) * math.log2(math.e)
MESH = pl.DeviceIdType.MESH
F32 = jnp.float32
BF16 = jnp.bfloat16


def dot_t(left, right):
    return lax.dot_general(left, right, (((1,), (1,)), ((), ())), preferred_element_type=F32)


def iota(shape, dimension):
    return lax.broadcasted_iota(jnp.int32, shape, dimension)


def block_stats(queries, keys, values, is_valid):
    scores = dot_t(queries, keys)
    if is_valid is not None:
        scores = jnp.where(is_valid, scores, NEG)
    peak = jnp.max(scores, axis=1, keepdims=True)
    weights = jnp.exp2((scores - peak) * EXP2_SCALE)
    if is_valid is not None:
        weights = jnp.where(is_valid, weights, 0.0)
    widened = jnp.concatenate([values, jnp.ones(values.shape, BF16)], axis=1)
    summed = jnp.dot(weights.astype(BF16), widened, preferred_element_type=F32)
    return peak, summed[:, :HEAD_DIMENSION], summed[:, HEAD_DIMENSION:]


def split(value):
    high = value.astype(BF16).astype(F32)
    low = (value - high).astype(BF16).astype(F32)
    return high, low, high + low


def pack(peaks, nums, dens):
    lane = iota((nums[0].shape[0], HEAD_DIMENSION), 1)
    stats = jnp.zeros(nums[0].shape, F32)
    for g in range(2):
        parts = (*split(peaks[g])[:2], *split(dens[g])[:2])
        for place, part in zip((2 * g, 2 * g + 1, 4 + 2 * g, 5 + 2 * g), parts):
            stats = jnp.where(lane == place, part, stats)
    return jnp.concatenate([nums[0], nums[1], stats], axis=1).astype(BF16)


def merge(messages):
    peaks, nums, dens = [], [], []
    stats = [message[:, 2 * HEAD_DIMENSION :].astype(F32) for message in messages]
    for g in range(2):
        tops = [stat[:, 2 * g : 2 * g + 1] + stat[:, 2 * g + 1 : 2 * g + 2] for stat in stats]
        peak = functools.reduce(jnp.maximum, tops)
        peak = split(peak)[2]
        num, den = 0.0, 0.0
        for message, stat, top in zip(messages, stats, tops):
            factor = jnp.exp2((top - peak) * EXP2_SCALE)
            den = den + factor * (stat[:, 4 + 2 * g : 5 + 2 * g] + stat[:, 5 + 2 * g : 6 + 2 * g])
            num = num + factor * message[
                :, g * HEAD_DIMENSION : (g + 1) * HEAD_DIMENSION
            ].astype(F32)
        peaks.append(peak)
        nums.append(num)
        dens.append(den)
    return peaks, nums, dens


def kernel(
    n_req,
    n_mp,
    q_hbm,
    fresh_hbm,
    suffix_hbm,
    length_hbm,
    prefix_hbm,
    owner_hbm,
    flag_hbm,
    panel_hbm,
    weight_hbm,
    out_ref,
    q_all,
    info_all,
    panel,
    suffix,
    fresh,
    length,
    prefix,
    owner,
    flag,
    weight,
    message_out,
    near_in,
    relay_in,
    final_out,
    final_in,
    attended,
    product,
    part_out,
    part_in,
    local_sem,
    q_send,
    q_recv,
    info_send,
    info_recv,
    forward_send,
    forward_recv,
    near_send,
    near_recv,
    relay_send,
    relay_recv,
    final_send,
    final_recv,
    part_send,
    part_recv,
):
    me = lax.axis_index("req")
    mp = lax.axis_index("mp")
    half = n_req // 2
    side = me // half
    place = me % half
    near_base = side * half
    far_base = (1 - side) * half
    counterpart = far_base + place
    kv_local = panel.shape[2] // HEAD_DIMENSION
    rows_rank = q_all.shape[1]
    slots = rows_rank // DECODE_STEPS
    rows = BLOCK_RANKS * rows_rank
    lanes = info_all.shape[2]

    local = [
        pltpu.make_async_copy(source, destination, local_sem.at[index])
        for index, (source, destination) in enumerate(
            [
                (flag_hbm, flag),
                (prefix_hbm, prefix),
                (length_hbm, length),
                (owner_hbm, owner),
                (q_hbm, q_all.at[me]),
                (panel_hbm, panel),
                (suffix_hbm, suffix),
                (fresh_hbm, fresh),
                (weight_hbm, weight),
            ]
        )
    ]
    for copy in local:
        copy.start()

    near = [(d, (place + d) % half, (place + half - d) % half) for d in range(1, half)]
    everyone = [
        (side_index * half + d, base + (place + d) % half, base + (place + half - d) % half)
        for side_index, base in ((1, far_base), (0, near_base))
        for d in range(1 - side_index, half)
    ]
    mp_peers = [(d, (mp + d) % n_mp, (mp + n_mp - d) % n_mp) for d in range(1, n_mp)]
    mp_peers = sorted(mp_peers, key=lambda peer: abs(peer[0] - n_mp // 2))

    barrier = pltpu.get_barrier_semaphore()
    for _, target, _ in everyone:
        pl.semaphore_signal(barrier, inc=1, device_id=(target, mp), device_id_type=MESH)
    for _, target, _ in mp_peers:
        pl.semaphore_signal(barrier, inc=1, device_id=(me, target), device_id_type=MESH)

    for copy in local[:4]:
        copy.wait()
    known = jnp.concatenate(
        [
            flag[...].astype(F32),
            prefix[...].astype(F32),
            jnp.zeros((8 - DECODE_STEPS - 1, slots), F32),
        ],
        axis=0,
    )
    lane = iota((8, lanes), 1)
    mine = jnp.zeros((8, lanes), F32)
    for k in range(slots):
        mine = jnp.where(lane == me * slots + k, known[:, k : k + 1], mine)
    info_all[me] = mine
    my_prefix = (owner[...] // 2).astype(F32)

    pl.semaphore_wait(barrier, n_req - 1 + n_mp - 1)

    def remote(source, destination, send, receive, device):
        return pltpu.make_async_remote_copy(
            src_ref=source,
            dst_ref=destination,
            send_sem=send,
            recv_sem=receive,
            device_id=device,
            device_id_type=MESH,
        )

    def info_copy(index, target, slot):
        return remote(
            info_all.at[me],
            info_all.at[slot],
            info_send.at[index],
            info_recv.at[index],
            (target, mp),
        )

    def query_copy(index, target, slot):
        return remote(
            q_hbm, q_all.at[slot], q_send.at[index], q_recv.at[index], (target, mp)
        )

    def forward_copy(index, target, slot):
        return remote(
            q_all.at[counterpart],
            q_all.at[slot],
            forward_send.at[index],
            forward_recv.at[index],
            (near_base + target, mp),
        )

    def near_copy(h, index, target, slot):
        return remote(
            message_out.at[h, near_base + target],
            near_in.at[h, slot],
            near_send.at[h, index],
            near_recv.at[h, index],
            (near_base + target, mp),
        )

    def relay_copy(h, index, target, slot):
        return remote(
            message_out.at[h, far_base + target],
            relay_in.at[h, slot],
            relay_send.at[h, index],
            relay_recv.at[h, index],
            (near_base + target, mp),
        )

    def final_copy(h):
        return remote(
            final_out.at[h], final_in.at[h], final_send.at[h], final_recv.at[h], (counterpart, mp)
        )

    def part_copy(index, target, slot):
        return remote(
            part_out.at[target],
            part_in.at[slot],
            part_send.at[index],
            part_recv.at[index],
            (me, target),
        )

    for index, target, _ in everyone:
        info_copy(index, target, me).start()
    query_copy(0, counterpart, me).start()
    for index, target, _ in near:
        query_copy(index, near_base + target, me).start()

    tokens = suffix.shape[1] * suffix.shape[2]
    column = jnp.where(
        iota((slots, slots), 0) == iota((slots, slots), 1),
        jnp.broadcast_to(length[...].astype(F32), (slots, slots)),
        0.0,
    )
    column = jnp.sum(column, axis=1, keepdims=True).astype(jnp.int32)
    slot = iota((slots, tokens), 1)
    live = (slot // SUFFIX_SLOTS == iota((slots, tokens), 0)) & (slot % SUFFIX_SLOTS < column)
    live = jnp.where(live, 1.0, 0.0)
    live = jnp.concatenate([live] * (2 * DECODE_STEPS), axis=0) > 0.5

    for index, target, source in everyone:
        info_copy(index, target, source).wait_recv()
    info = info_all[0]
    for rank in range(1, n_req):
        info = info + info_all[rank]
    state_row = iota((8, lanes), 0)
    position = iota((8, lanes), 1)
    state = jnp.where(
        state_row == 0,
        position.astype(F32),
        jnp.where(state_row == 1, jnp.broadcast_to(info[4:5], (8, lanes)), 0.0),
    )
    bit_count = n_req.bit_length() - 1
    requests = jnp.zeros((8, lanes), F32)
    for step in range(DECODE_STEPS):
        distance = slots << (step % bit_count)
        lane = iota((lanes, lanes), 1)
        partner = jnp.where((lane // distance) % 2 == 1, lane - distance, lane + distance)
        flagged = jnp.broadcast_to(info[step : step + 1], (lanes, lanes)) > 0.5
        origin = jnp.where(flagged, partner, lane)
        moves = jnp.where(iota((lanes, lanes), 0) == origin, 1.0, 0.0).astype(BF16)
        state = jnp.dot(state.astype(BF16), moves, preferred_element_type=F32)
        requests = jnp.where(state_row == step, state[0:1], requests)
        requests = jnp.where(state_row == DECODE_STEPS + step, state[1:2], requests)
    requests = requests.astype(BF16)
    token = iota((rows_rank, lanes), 0)
    token_at = jnp.where(iota((rows_rank, lanes), 1) == me * slots + token % slots, 1.0, 0.0)
    token_steps = dot_t(requests, token_at.astype(BF16))
    token_step = iota((1, rows_rank), 1) // slots
    token_request = jnp.zeros((1, rows_rank), F32)
    for step in range(DECODE_STEPS):
        token_request = jnp.where(token_step == step, token_steps[step : step + 1], token_request)

    def prepare(first):
        row = iota((rows, lanes), 0)
        row_position = (first + row // rows_rank) * slots + row % slots
        row_at = jnp.where(iota((rows, lanes), 1) == row_position, 1.0, 0.0).astype(BF16)
        down = dot_t(row_at, requests)
        across = dot_t(requests, row_at)
        down_step = (iota((rows, 1), 0) // slots) % DECODE_STEPS
        across_step = (iota((1, rows), 1) // slots) % DECODE_STEPS
        down_request = jnp.zeros((rows, 1), F32)
        down_prefix = jnp.zeros((rows, 1), F32)
        across_request = jnp.zeros((1, rows), F32)
        for step in range(DECODE_STEPS):
            here = down_step == step
            down_request = jnp.where(here, down[:, step : step + 1], down_request)
            down_prefix = jnp.where(
                here, down[:, DECODE_STEPS + step : DECODE_STEPS + step + 1], down_prefix
            )
            across_request = jnp.where(across_step == step, across[step : step + 1], across_request)
        matched = jnp.where(down_prefix == my_prefix, 1.0, 0.0)
        matched = jnp.concatenate([matched, matched], axis=0) > 0.5
        own = iota((rows_rank, rows), 0)
        pick = jnp.where(
            (across_request == (me * slots + own % slots).astype(F32))
            & (across_step == own // slots),
            1.0,
            0.0,
        ).astype(BF16)
        own = iota((rows, rows_rank), 1)
        put = jnp.where(
            (down_request == (me * slots + own % slots).astype(F32)) & (down_step == own // slots),
            1.0,
            0.0,
        )
        is_here = jnp.sum(put, axis=1, keepdims=True)
        is_here = jnp.concatenate([is_here, is_here], axis=0) > 0.5
        fresh_valid = jnp.where(
            (down_request == token_request) & (down_step >= token_step), 1.0, 0.0
        )
        fresh_valid = jnp.concatenate([fresh_valid, fresh_valid], axis=0) > 0.5
        return first, matched, pick, put, is_here, fresh_valid

    def head(h, prepared):
        first, matched, pick, put, is_here, fresh_valid = prepared
        at = slice(h * HEAD_DIMENSION, (h + 1) * HEAD_DIMENSION)
        query = [
            q_all[
                pl.ds(first, BLOCK_RANKS),
                :,
                (2 * h + g) * HEAD_DIMENSION : (2 * h + g + 1) * HEAD_DIMENSION,
            ].reshape(rows, HEAD_DIMENSION)
            for g in range(2)
        ]
        both = jnp.concatenate(query, axis=0)
        panel_peak, panel_num, panel_den = block_stats(
            both, panel[0, :, at], panel[1, :, at], None
        )
        panel_peak = jnp.where(matched, panel_peak, NEG)
        own_query = jnp.concatenate(
            [jnp.dot(pick, part, preferred_element_type=F32) for part in query], axis=0
        ).astype(BF16)
        own_peak, own_num, own_den = block_stats(
            own_query,
            suffix[0, :, :, at].reshape(tokens, HEAD_DIMENSION),
            suffix[1, :, :, at].reshape(tokens, HEAD_DIMENSION),
            live,
        )
        own_all = jnp.concatenate(
            [own_num, own_den, jnp.broadcast_to(own_peak, own_num.shape)], axis=1
        )
        own_all = jnp.concatenate(
            [
                jnp.dot(
                    put,
                    own_all[g * rows_rank : (g + 1) * rows_rank],
                    preferred_element_type=F32,
                    precision=lax.Precision.HIGHEST,
                )
                for g in range(2)
            ],
            axis=0,
        )
        own_num = own_all[:, :HEAD_DIMENSION]
        own_den = own_all[:, HEAD_DIMENSION : 2 * HEAD_DIMENSION]
        own_peak = jnp.where(is_here, own_all[:, 2 * HEAD_DIMENSION :], NEG)
        fresh_peak, fresh_num, fresh_den = block_stats(
            both, fresh[0, :, at], fresh[1, :, at], fresh_valid
        )
        peak = jnp.maximum(jnp.maximum(panel_peak, fresh_peak), own_peak)
        peak = split(peak)[2]
        panel_factor = jnp.where(matched, jnp.exp2((panel_peak - peak) * EXP2_SCALE), 0.0)
        own_factor = jnp.exp2((own_peak - peak) * EXP2_SCALE)
        fresh_factor = jnp.exp2((fresh_peak - peak) * EXP2_SCALE)
        num = panel_num * panel_factor + own_num * own_factor + fresh_num * fresh_factor
        den = panel_den * panel_factor + own_den * own_factor + fresh_den * fresh_factor
        message = pack(
            [peak[:rows], peak[rows:]], [num[:rows], num[rows:]], [den[:rows], den[rows:]]
        )
        message_out[h, pl.ds(first, BLOCK_RANKS)] = message.reshape(
            BLOCK_RANKS, rows_rank, 3 * HEAD_DIMENSION
        )

    def near_head(h):
        for prepared in near_rows:
            head(h, prepared)
        for index, target, _ in near:
            near_copy(h, index, target, place).start()

    def far_head(h):
        for prepared in far_rows:
            head(h, prepared)
        for index, target, _ in near:
            relay_copy(h, index, target, place).start()

    def relay(h):
        for index, target, source in near:
            relay_copy(h, index, target, source).wait_recv()
        messages = [message_out[h, counterpart]]
        messages += [relay_in[h, source] for _, _, source in near]
        final_out[h] = pack(*merge(messages))
        final_copy(h).start()

    def attend(h):
        for index, target, source in near:
            near_copy(h, index, target, source).wait_recv()
        final_copy(h).wait_recv()
        messages = [message_out[h, me], final_in[h]]
        messages += [near_in[h, source] for _, _, source in near]
        _, nums, dens = merge(messages)
        for g in range(2):
            at = slice((2 * h + g) * HEAD_DIMENSION, (2 * h + g + 1) * HEAD_DIMENSION)
            attended[:, at] = (nums[g] / dens[g]).astype(BF16)

    blocks = range(half // BLOCK_RANKS)
    near_rows = [prepare(near_base + block * BLOCK_RANKS) for block in blocks]
    query_copy(0, counterpart, counterpart).wait_recv()
    for index, target, _ in near:
        forward_copy(index, target, counterpart).start()
    for copy in local[4:8]:
        copy.wait()
    for index, target, source in near:
        query_copy(index, near_base + target, near_base + source).wait_recv()
    early = kv_local // 2
    for h in range(early):
        near_head(h)
    far_rows = [prepare(far_base + block * BLOCK_RANKS) for block in blocks]
    for index, target, source in near:
        forward_copy(index, target, far_base + source).wait_recv()
    for h in range(kv_local):
        far_head(h)
        if h:
            relay(h - 1)
    for h in range(early, kv_local):
        near_head(h)
        if h == early:
            relay(kv_local - 1)
    for h in range(kv_local - 1):
        attend(h)

    local[8].wait()
    width = out_ref.shape[1]
    known_lanes = (kv_local - 1) * 2 * HEAD_DIMENSION

    def project(target, rows_from, rows_to):
        columns = pl.ds(pl.multiple_of(target * width, HEAD_DIMENSION), width)
        return jnp.dot(
            attended[:, rows_from:rows_to],
            weight[rows_from:rows_to, columns],
            preferred_element_type=F32,
        )

    targets = [target for _, target, _ in mp_peers] + [mp]
    for order, target in enumerate(targets):
        product[order] = project(target, 0, known_lanes)
    attend(kv_local - 1)
    for order, (index, target, _) in enumerate(mp_peers):
        total = product[order] + project(target, known_lanes, attended.shape[1])
        part_out[target] = total.astype(BF16)
        part_copy(index, target, mp).start()
    result = product[n_mp - 1] + project(mp, known_lanes, attended.shape[1])
    for index, target, source in mp_peers:
        part_copy(index, target, source).wait_recv()
        result = result + part_in[source].astype(F32)
    out_ref[...] = result.astype(BF16)

    for index, target, source in everyone:
        info_copy(index, target, source).wait_send()
    query_copy(0, counterpart, counterpart).wait_send()
    for index, target, source in near:
        query_copy(index, near_base + target, near_base + source).wait_send()
        forward_copy(index, target, far_base + source).wait_send()
    for h in range(kv_local):
        for index, target, source in near:
            near_copy(h, index, target, source).wait_send()
            relay_copy(h, index, target, source).wait_send()
        final_copy(h).wait_send()
    for index, target, source in mp_peers:
        part_copy(index, target, source).wait_send()


def shards(
    queries,
    fresh_key_value,
    suffix_key_value,
    suffix_len,
    prefix_ids,
    panel_owner,
    prefix_key_value,
    out_weight,
    swap_flags,
):
    n_req = lax.axis_size("req")
    n_mp = lax.axis_size("mp")
    half = n_req // 2
    slots = queries.shape[1]
    rows_rank = DECODE_STEPS * slots
    model_lanes = queries.shape[2]
    kv_lanes = suffix_key_value.shape[3]
    kv_local = kv_lanes // HEAD_DIMENSION
    width = out_weight.shape[1] // n_mp
    lanes = max(128, n_req * slots)
    message = 3 * HEAD_DIMENSION
    anywhere = pl.BlockSpec(memory_space=pl.ANY)
    dma = pltpu.SemaphoreType.DMA
    out = pl.pallas_call(
        functools.partial(kernel, n_req, n_mp),
        out_shape=jax.ShapeDtypeStruct((rows_rank, width), BF16),
        in_specs=[anywhere] * 9,
        out_specs=pl.BlockSpec(memory_space=pltpu.VMEM),
        scratch_shapes=[
            pltpu.VMEM((n_req, rows_rank, model_lanes), BF16),
            pltpu.VMEM((n_req, 8, lanes), F32),
            pltpu.VMEM((2, PANEL_TOKENS, kv_lanes), BF16),
            pltpu.VMEM((2, slots, SUFFIX_SLOTS, kv_lanes), BF16),
            pltpu.VMEM((2, rows_rank, kv_lanes), BF16),
            pltpu.VMEM((1, slots), jnp.int32),
            pltpu.VMEM((1, slots), jnp.int32),
            pltpu.VMEM((1, 1), jnp.int32),
            pltpu.VMEM((DECODE_STEPS, slots), jnp.int32),
            pltpu.VMEM(out_weight.shape, BF16),
            pltpu.VMEM((kv_local, n_req, rows_rank, message), BF16),
            pltpu.VMEM((kv_local, half, rows_rank, message), BF16),
            pltpu.VMEM((kv_local, half, rows_rank, message), BF16),
            pltpu.VMEM((kv_local, rows_rank, message), BF16),
            pltpu.VMEM((kv_local, rows_rank, message), BF16),
            pltpu.VMEM((rows_rank, model_lanes), BF16),
            pltpu.VMEM((n_mp, rows_rank, width), F32),
            pltpu.VMEM((n_mp, rows_rank, width), BF16),
            pltpu.VMEM((n_mp, rows_rank, width), BF16),
            dma((9,)),
        ]
        + [dma((half,))] * 2
        + [dma((n_req,))] * 2
        + [dma((half,))] * 2
        + [dma((kv_local, half))] * 4
        + [dma((kv_local,))] * 2
        + [dma((n_mp,))] * 2,
        compiler_params=pltpu.CompilerParams(
            collective_id=0, has_side_effects=True, vmem_limit_bytes=56 * 2**20
        ),
        name="cascade",
    )(
        queries.reshape(rows_rank, model_lanes),
        fresh_key_value.transpose(1, 0, 2, 3).reshape(2, rows_rank, kv_lanes),
        suffix_key_value,
        suffix_len.reshape(1, slots),
        prefix_ids.reshape(1, slots),
        panel_owner.reshape(1, 1),
        swap_flags,
        prefix_key_value.reshape(2, PANEL_TOKENS, kv_lanes),
        out_weight,
    )
    return out.reshape(DECODE_STEPS, slots, width)


def solution(mesh):
    placed = (
        P(None, "req", "mp"),
        P(None, None, "req", "mp"),
        P(None, "req", None, "mp"),
        P("req"),
        P("req"),
        P("req"),
        P(None, "req", None, "mp"),
        P("mp", None),
        P(None, "req"),
    )
    return jax.shard_map(
        shards, mesh=mesh, in_specs=placed, out_specs=P(None, "req", "mp"), check_vma=False
    )
```

```python
import functools
import math

import jax
import jax.numpy as jnp
from jax import lax
from jax.experimental import pallas as pl
from jax.experimental.pallas import tpu as pltpu
from jax.sharding import PartitionSpec as P

D = 4608
QUERY_HEADS = 32
HEAD_DIMENSION = 128
SUFFIX_SLOTS = 128
PANEL_TOKENS = 2048
DECODE_STEPS = 4
BLOCK_RANKS = 4

NEG = -(2.0**100)
EXP2_SCALE = (D // QUERY_HEADS) ** (-0.5) * math.log2(math.e)
MESH = pl.DeviceIdType.MESH
F32 = jnp.float32
BF16 = jnp.bfloat16


def dot_t(left, right):
    return lax.dot_general(left, right, (((1,), (1,)), ((), ())), preferred_element_type=F32)


def iota(shape, dimension):
    return lax.broadcasted_iota(jnp.int32, shape, dimension)


def block_stats(queries, keys, values, is_valid):
    scores = dot_t(queries, keys)
    if is_valid is not None:
        scores = jnp.where(is_valid, scores, NEG)
    peak = jnp.max(scores, axis=1, keepdims=True)
    weights = jnp.exp2((scores - peak) * EXP2_SCALE)
    if is_valid is not None:
        weights = jnp.where(is_valid, weights, 0.0)
    widened = jnp.concatenate([values, jnp.ones(values.shape, BF16)], axis=1)
    summed = jnp.dot(weights.astype(BF16), widened, preferred_element_type=F32)
    return peak, summed[:, :HEAD_DIMENSION], summed[:, HEAD_DIMENSION:]


def split(value):
    high = value.astype(BF16).astype(F32)
    low = (value - high).astype(BF16).astype(F32)
    return high, low, high + low


def three_parts(value):
    high = value.astype(BF16).astype(F32)
    rest = value - high
    middle = rest.astype(BF16).astype(F32)
    return jnp.concatenate([high, middle, rest - middle], axis=0).astype(BF16)


def pack(peaks, nums, dens):
    lane = iota((nums[0].shape[0], HEAD_DIMENSION), 1)
    stats = jnp.zeros(nums[0].shape, F32)
    for g in range(2):
        parts = (*split(peaks[g])[:2], *split(dens[g])[:2])
        for place, part in zip((2 * g, 2 * g + 1, 4 + 2 * g, 5 + 2 * g), parts):
            stats = jnp.where(lane == place, part, stats)
    return jnp.concatenate([nums[0], nums[1], stats], axis=1).astype(BF16)


def merge(messages):
    peaks, nums, dens = [], [], []
    stats = [message[:, 2 * HEAD_DIMENSION :].astype(F32) for message in messages]
    for g in range(2):
        tops = [stat[:, 2 * g : 2 * g + 1] + stat[:, 2 * g + 1 : 2 * g + 2] for stat in stats]
        peak = functools.reduce(jnp.maximum, tops)
        peak = split(peak)[2]
        num, den = 0.0, 0.0
        for message, stat, top in zip(messages, stats, tops):
            factor = jnp.exp2((top - peak) * EXP2_SCALE)
            den = den + factor * (stat[:, 4 + 2 * g : 5 + 2 * g] + stat[:, 5 + 2 * g : 6 + 2 * g])
            num = num + factor * message[
                :, g * HEAD_DIMENSION : (g + 1) * HEAD_DIMENSION
            ].astype(F32)
        peaks.append(peak)
        nums.append(num)
        dens.append(den)
    return peaks, nums, dens


def kernel(
    n_req,
    n_mp,
    q_hbm,
    fresh_hbm,
    suffix_hbm,
    length_hbm,
    prefix_hbm,
    owner_hbm,
    flag_hbm,
    panel_hbm,
    weight_hbm,
    out_ref,
    q_all,
    info_all,
    panel,
    suffix,
    fresh,
    length,
    prefix,
    owner,
    flag,
    weight,
    message_out,
    near_in,
    relay_in,
    final_out,
    final_in,
    attended,
    product,
    part_out,
    part_in,
    local_sem,
    q_send,
    q_recv,
    info_send,
    info_recv,
    forward_send,
    forward_recv,
    near_send,
    near_recv,
    relay_send,
    relay_recv,
    final_send,
    final_recv,
    part_send,
    part_recv,
):
    me = lax.axis_index("req")
    mp = lax.axis_index("mp")
    half = n_req // 2
    side = me // half
    place = me % half
    near_base = side * half
    far_base = (1 - side) * half
    counterpart = far_base + place
    kv_local = panel.shape[2] // HEAD_DIMENSION
    rows_rank = q_all.shape[1]
    slots = rows_rank // DECODE_STEPS
    rows = BLOCK_RANKS * rows_rank
    lanes = info_all.shape[2]

    local = [
        pltpu.make_async_copy(source, destination, local_sem.at[index])
        for index, (source, destination) in enumerate(
            [
                (flag_hbm, flag),
                (prefix_hbm, prefix),
                (length_hbm, length),
                (owner_hbm, owner),
                (q_hbm, q_all.at[me]),
                (panel_hbm, panel),
                (suffix_hbm, suffix),
                (fresh_hbm, fresh),
                (weight_hbm, weight),
            ]
        )
    ]
    for copy in local:
        copy.start()

    near = [(d, (place + d) % half, (place + half - d) % half) for d in range(1, half)]
    everyone = [
        (side_index * half + d, base + (place + d) % half, base + (place + half - d) % half)
        for side_index, base in ((1, far_base), (0, near_base))
        for d in range(1 - side_index, half)
    ]
    mp_peers = [(d, (mp + d) % n_mp, (mp + n_mp - d) % n_mp) for d in range(1, n_mp)]
    mp_peers = sorted(mp_peers, key=lambda peer: abs(peer[0] - n_mp // 2))

    barrier = pltpu.get_barrier_semaphore()
    for _, target, _ in everyone:
        pl.semaphore_signal(barrier, inc=1, device_id=(target, mp), device_id_type=MESH)
    for _, target, _ in mp_peers:
        pl.semaphore_signal(barrier, inc=1, device_id=(me, target), device_id_type=MESH)

    for copy in local[:4]:
        copy.wait()
    known = jnp.concatenate(
        [
            flag[...].astype(F32),
            prefix[...].astype(F32),
            jnp.zeros((8 - DECODE_STEPS - 1, slots), F32),
        ],
        axis=0,
    )
    lane = iota((8, lanes), 1)
    mine = jnp.zeros((8, lanes), F32)
    for k in range(slots):
        mine = jnp.where(lane == me * slots + k, known[:, k : k + 1], mine)
    info_all[me] = mine
    my_prefix = (owner[...] // 2).astype(F32)

    pl.semaphore_wait(barrier, n_req - 1 + n_mp - 1)

    def remote(source, destination, send, receive, device):
        return pltpu.make_async_remote_copy(
            src_ref=source,
            dst_ref=destination,
            send_sem=send,
            recv_sem=receive,
            device_id=device,
            device_id_type=MESH,
        )

    def info_copy(index, target, slot):
        return remote(
            info_all.at[me],
            info_all.at[slot],
            info_send.at[index],
            info_recv.at[index],
            (target, mp),
        )

    def query_copy(index, target, slot):
        return remote(
            q_hbm, q_all.at[slot], q_send.at[index], q_recv.at[index], (target, mp)
        )

    def forward_copy(index, target, slot):
        return remote(
            q_all.at[counterpart],
            q_all.at[slot],
            forward_send.at[index],
            forward_recv.at[index],
            (near_base + target, mp),
        )

    def near_copy(h, index, target, slot):
        return remote(
            message_out.at[h, near_base + target],
            near_in.at[h, slot],
            near_send.at[h, index],
            near_recv.at[h, index],
            (near_base + target, mp),
        )

    def relay_copy(h, index, target, slot):
        return remote(
            message_out.at[h, far_base + target],
            relay_in.at[h, slot],
            relay_send.at[h, index],
            relay_recv.at[h, index],
            (near_base + target, mp),
        )

    def final_copy(h):
        return remote(
            final_out.at[h], final_in.at[h], final_send.at[h], final_recv.at[h], (counterpart, mp)
        )

    def part_copy(index, target, slot):
        return remote(
            part_out.at[target],
            part_in.at[slot],
            part_send.at[index],
            part_recv.at[index],
            (me, target),
        )

    for index, target, _ in everyone:
        info_copy(index, target, me).start()
    query_copy(0, counterpart, me).start()
    for index, target, _ in near:
        query_copy(index, near_base + target, me).start()

    tokens = suffix.shape[1] * suffix.shape[2]
    column = jnp.where(
        iota((slots, slots), 0) == iota((slots, slots), 1),
        jnp.broadcast_to(length[...].astype(F32), (slots, slots)),
        0.0,
    )
    column = jnp.sum(column, axis=1, keepdims=True).astype(jnp.int32)
    slot = iota((slots, tokens), 1)
    live = (slot // SUFFIX_SLOTS == iota((slots, tokens), 0)) & (slot % SUFFIX_SLOTS < column)
    live = jnp.where(live, 1.0, 0.0)
    live = jnp.concatenate([live] * (2 * DECODE_STEPS), axis=0) > 0.5

    for index, target, source in everyone:
        info_copy(index, target, source).wait_recv()
    info = info_all[0]
    for rank in range(1, n_req):
        info = info + info_all[rank]
    state_row = iota((8, lanes), 0)
    position = iota((8, lanes), 1)
    state = jnp.where(
        state_row == 0,
        position.astype(F32),
        jnp.where(state_row == 1, jnp.broadcast_to(info[4:5], (8, lanes)), 0.0),
    )
    bit_count = n_req.bit_length() - 1
    requests = jnp.zeros((8, lanes), F32)
    for step in range(DECODE_STEPS):
        distance = slots << (step % bit_count)
        lane = iota((lanes, lanes), 1)
        partner = jnp.where((lane // distance) % 2 == 1, lane - distance, lane + distance)
        flagged = jnp.broadcast_to(info[step : step + 1], (lanes, lanes)) > 0.5
        origin = jnp.where(flagged, partner, lane)
        moves = jnp.where(iota((lanes, lanes), 0) == origin, 1.0, 0.0).astype(BF16)
        state = jnp.dot(state.astype(BF16), moves, preferred_element_type=F32)
        requests = jnp.where(state_row == step, state[0:1], requests)
        requests = jnp.where(state_row == DECODE_STEPS + step, state[1:2], requests)
    requests = requests.astype(BF16)
    token = iota((rows_rank, lanes), 0)
    token_at = jnp.where(iota((rows_rank, lanes), 1) == me * slots + token % slots, 1.0, 0.0)
    token_steps = dot_t(requests, token_at.astype(BF16))
    token_step = iota((1, rows_rank), 1) // slots
    token_request = jnp.zeros((1, rows_rank), F32)
    for step in range(DECODE_STEPS):
        token_request = jnp.where(token_step == step, token_steps[step : step + 1], token_request)

    def prepare(first):
        row = iota((rows, lanes), 0)
        row_position = (first + row // rows_rank) * slots + row % slots
        row_at = jnp.where(iota((rows, lanes), 1) == row_position, 1.0, 0.0).astype(BF16)
        down = dot_t(row_at, requests)
        across = dot_t(requests, row_at)
        down_step = (iota((rows, 1), 0) // slots) % DECODE_STEPS
        across_step = (iota((1, rows), 1) // slots) % DECODE_STEPS
        down_request = jnp.zeros((rows, 1), F32)
        down_prefix = jnp.zeros((rows, 1), F32)
        across_request = jnp.zeros((1, rows), F32)
        for step in range(DECODE_STEPS):
            here = down_step == step
            down_request = jnp.where(here, down[:, step : step + 1], down_request)
            down_prefix = jnp.where(
                here, down[:, DECODE_STEPS + step : DECODE_STEPS + step + 1], down_prefix
            )
            across_request = jnp.where(across_step == step, across[step : step + 1], across_request)
        matched = jnp.where(down_prefix == my_prefix, 1.0, 0.0)
        matched = jnp.concatenate([matched, matched], axis=0) > 0.5
        own = iota((rows_rank, rows), 0)
        pick = jnp.where(
            (across_request == (me * slots + own % slots).astype(F32))
            & (across_step == own // slots),
            1.0,
            0.0,
        ).astype(BF16)
        own = iota((rows, rows_rank), 1)
        put = jnp.where(
            (down_request == (me * slots + own % slots).astype(F32)) & (down_step == own // slots),
            1.0,
            0.0,
        )
        is_here = jnp.sum(put, axis=1, keepdims=True)
        is_here = jnp.concatenate([is_here, is_here], axis=0) > 0.5
        fresh_valid = jnp.where(
            (down_request == token_request) & (down_step >= token_step), 1.0, 0.0
        )
        fresh_valid = jnp.concatenate([fresh_valid, fresh_valid], axis=0) > 0.5
        return first, matched, pick, put, is_here, fresh_valid

    def head(h, prepared):
        first, matched, pick, put, is_here, fresh_valid = prepared
        at = slice(h * HEAD_DIMENSION, (h + 1) * HEAD_DIMENSION)
        query = [
            q_all[
                pl.ds(first, BLOCK_RANKS),
                :,
                (2 * h + g) * HEAD_DIMENSION : (2 * h + g + 1) * HEAD_DIMENSION,
            ].reshape(rows, HEAD_DIMENSION)
            for g in range(2)
        ]
        both = jnp.concatenate(query, axis=0)
        panel_peak, panel_num, panel_den = block_stats(
            both, panel[0, :, at], panel[1, :, at], None
        )
        panel_peak = jnp.where(matched, panel_peak, NEG)
        own_query = jnp.concatenate(
            [jnp.dot(pick, part, preferred_element_type=F32) for part in query], axis=0
        ).astype(BF16)
        own_peak, own_num, own_den = block_stats(
            own_query,
            suffix[0, :, :, at].reshape(tokens, HEAD_DIMENSION),
            suffix[1, :, :, at].reshape(tokens, HEAD_DIMENSION),
            live,
        )
        put_thrice = jnp.concatenate([put, put, put], axis=1).astype(BF16)
        own_all = jnp.concatenate(
            [own_num, own_den, jnp.broadcast_to(own_peak, own_num.shape)], axis=1
        )
        own_all = jnp.concatenate(
            [
                jnp.dot(
                    put_thrice,
                    three_parts(own_all[g * rows_rank : (g + 1) * rows_rank]),
                    preferred_element_type=F32,
                )
                for g in range(2)
            ],
            axis=0,
        )
        own_num = own_all[:, :HEAD_DIMENSION]
        own_den = own_all[:, HEAD_DIMENSION : 2 * HEAD_DIMENSION]
        own_peak = jnp.where(is_here, own_all[:, 2 * HEAD_DIMENSION :], NEG)
        fresh_peak, fresh_num, fresh_den = block_stats(
            both, fresh[0, :, at], fresh[1, :, at], fresh_valid
        )
        peak = jnp.maximum(jnp.maximum(panel_peak, fresh_peak), own_peak)
        peak = split(peak)[2]
        panel_factor = jnp.where(matched, jnp.exp2((panel_peak - peak) * EXP2_SCALE), 0.0)
        own_factor = jnp.exp2((own_peak - peak) * EXP2_SCALE)
        fresh_factor = jnp.exp2((fresh_peak - peak) * EXP2_SCALE)
        num = panel_num * panel_factor + own_num * own_factor + fresh_num * fresh_factor
        den = panel_den * panel_factor + own_den * own_factor + fresh_den * fresh_factor
        message = pack(
            [peak[:rows], peak[rows:]], [num[:rows], num[rows:]], [den[:rows], den[rows:]]
        )
        message_out[h, pl.ds(first, BLOCK_RANKS)] = message.reshape(
            BLOCK_RANKS, rows_rank, 3 * HEAD_DIMENSION
        )

    def near_head(h):
        for prepared in near_rows:
            head(h, prepared)
        for index, target, _ in near:
            near_copy(h, index, target, place).start()

    def far_head(h):
        for prepared in far_rows:
            head(h, prepared)
        for index, target, _ in near:
            relay_copy(h, index, target, place).start()

    def relay(h):
        for index, target, source in near:
            relay_copy(h, index, target, source).wait_recv()
        messages = [message_out[h, counterpart]]
        messages += [relay_in[h, source] for _, _, source in near]
        final_out[h] = pack(*merge(messages))
        final_copy(h).start()

    def attend(h):
        for index, target, source in near:
            near_copy(h, index, target, source).wait_recv()
        final_copy(h).wait_recv()
        messages = [message_out[h, me], final_in[h]]
        messages += [near_in[h, source] for _, _, source in near]
        _, nums, dens = merge(messages)
        for g in range(2):
            at = slice((2 * h + g) * HEAD_DIMENSION, (2 * h + g + 1) * HEAD_DIMENSION)
            attended[:, at] = (nums[g] / dens[g]).astype(BF16)

    blocks = range(half // BLOCK_RANKS)
    near_rows = [prepare(near_base + block * BLOCK_RANKS) for block in blocks]
    query_copy(0, counterpart, counterpart).wait_recv()
    for index, target, _ in near:
        forward_copy(index, target, counterpart).start()
    for copy in local[4:8]:
        copy.wait()
    for index, target, source in near:
        query_copy(index, near_base + target, near_base + source).wait_recv()
    early = kv_local // 2
    for h in range(early):
        near_head(h)
    far_rows = [prepare(far_base + block * BLOCK_RANKS) for block in blocks]
    for index, target, source in near:
        forward_copy(index, target, far_base + source).wait_recv()
    for h in range(kv_local):
        far_head(h)
        if h:
            relay(h - 1)
    for h in range(early, kv_local):
        near_head(h)
        if h == early:
            relay(kv_local - 1)
    for h in range(kv_local - 1):
        attend(h)

    local[8].wait()
    width = out_ref.shape[1]
    known_lanes = (kv_local - 1) * 2 * HEAD_DIMENSION

    def project(target, rows_from, rows_to):
        columns = pl.ds(pl.multiple_of(target * width, HEAD_DIMENSION), width)
        return jnp.dot(
            attended[:, rows_from:rows_to],
            weight[rows_from:rows_to, columns],
            preferred_element_type=F32,
        )

    targets = [target for _, target, _ in mp_peers] + [mp]
    for order, target in enumerate(targets):
        product[order] = project(target, 0, known_lanes)
    attend(kv_local - 1)
    for order, (index, target, _) in enumerate(mp_peers):
        total = product[order] + project(target, known_lanes, attended.shape[1])
        part_out[target] = total.astype(BF16)
        part_copy(index, target, mp).start()
    result = product[n_mp - 1] + project(mp, known_lanes, attended.shape[1])
    for index, target, source in mp_peers:
        part_copy(index, target, source).wait_recv()
        result = result + part_in[source].astype(F32)
    out_ref[...] = result.astype(BF16)

    for index, target, source in everyone:
        info_copy(index, target, source).wait_send()
    query_copy(0, counterpart, counterpart).wait_send()
    for index, target, source in near:
        query_copy(index, near_base + target, near_base + source).wait_send()
        forward_copy(index, target, far_base + source).wait_send()
    for h in range(kv_local):
        for index, target, source in near:
            near_copy(h, index, target, source).wait_send()
            relay_copy(h, index, target, source).wait_send()
        final_copy(h).wait_send()
    for index, target, source in mp_peers:
        part_copy(index, target, source).wait_send()


def shards(
    queries,
    fresh_key_value,
    suffix_key_value,
    suffix_len,
    prefix_ids,
    panel_owner,
    prefix_key_value,
    out_weight,
    swap_flags,
):
    n_req = lax.axis_size("req")
    n_mp = lax.axis_size("mp")
    half = n_req // 2
    slots = queries.shape[1]
    rows_rank = DECODE_STEPS * slots
    model_lanes = queries.shape[2]
    kv_lanes = suffix_key_value.shape[3]
    kv_local = kv_lanes // HEAD_DIMENSION
    width = out_weight.shape[1] // n_mp
    lanes = max(128, n_req * slots)
    message = 3 * HEAD_DIMENSION
    anywhere = pl.BlockSpec(memory_space=pl.ANY)
    dma = pltpu.SemaphoreType.DMA
    out = pl.pallas_call(
        functools.partial(kernel, n_req, n_mp),
        out_shape=jax.ShapeDtypeStruct((rows_rank, width), BF16),
        in_specs=[anywhere] * 9,
        out_specs=pl.BlockSpec(memory_space=pltpu.VMEM),
        scratch_shapes=[
            pltpu.VMEM((n_req, rows_rank, model_lanes), BF16),
            pltpu.VMEM((n_req, 8, lanes), F32),
            pltpu.VMEM((2, PANEL_TOKENS, kv_lanes), BF16),
            pltpu.VMEM((2, slots, SUFFIX_SLOTS, kv_lanes), BF16),
            pltpu.VMEM((2, rows_rank, kv_lanes), BF16),
            pltpu.VMEM((1, slots), jnp.int32),
            pltpu.VMEM((1, slots), jnp.int32),
            pltpu.VMEM((1, 1), jnp.int32),
            pltpu.VMEM((DECODE_STEPS, slots), jnp.int32),
            pltpu.VMEM(out_weight.shape, BF16),
            pltpu.VMEM((kv_local, n_req, rows_rank, message), BF16),
            pltpu.VMEM((kv_local, half, rows_rank, message), BF16),
            pltpu.VMEM((kv_local, half, rows_rank, message), BF16),
            pltpu.VMEM((kv_local, rows_rank, message), BF16),
            pltpu.VMEM((kv_local, rows_rank, message), BF16),
            pltpu.VMEM((rows_rank, model_lanes), BF16),
            pltpu.VMEM((n_mp, rows_rank, width), F32),
            pltpu.VMEM((n_mp, rows_rank, width), BF16),
            pltpu.VMEM((n_mp, rows_rank, width), BF16),
            dma((9,)),
        ]
        + [dma((half,))] * 2
        + [dma((n_req,))] * 2
        + [dma((half,))] * 2
        + [dma((kv_local, half))] * 4
        + [dma((kv_local,))] * 2
        + [dma((n_mp,))] * 2,
        compiler_params=pltpu.CompilerParams(
            collective_id=0, has_side_effects=True, vmem_limit_bytes=56 * 2**20
        ),
        name="cascade",
    )(
        queries.reshape(rows_rank, model_lanes),
        fresh_key_value.transpose(1, 0, 2, 3).reshape(2, rows_rank, kv_lanes),
        suffix_key_value,
        suffix_len.reshape(1, slots),
        prefix_ids.reshape(1, slots),
        panel_owner.reshape(1, 1),
        swap_flags,
        prefix_key_value.reshape(2, PANEL_TOKENS, kv_lanes),
        out_weight,
    )
    return out.reshape(DECODE_STEPS, slots, width)


def solution(mesh):
    placed = (
        P(None, "req", "mp"),
        P(None, None, "req", "mp"),
        P(None, "req", None, "mp"),
        P("req"),
        P("req"),
        P("req"),
        P(None, "req", None, "mp"),
        P("mp", None),
        P(None, "req"),
    )
    return jax.shard_map(
        shards, mesh=mesh, in_specs=placed, out_specs=P(None, "req", "mp"), check_vma=False
    )
```
